512 devices in a mesh: pipe: 32 (over z_lo, y, core), tensor: 16 (over z_hi, x).
Axes of the slice: x: 4, y: 4, z: 16 (z_hi: 4, z_lo: 4; z = z_hi * 4 + z_lo), core: 2. Of those that a mesh axis runs over, the one named last changes fastest.
Arguments:
- fwd_qkv: bfloat16 [32, 896, 32, 384], P('pipe', None, 'tensor'), may hold values from -5 to 5
- held_stash: bfloat16 [32, 896, 32, 384], P('pipe', 'tensor'), may hold values from -5 to 5
- d_out: bfloat16 [32, 896, 32, 128], P('pipe', None, 'tensor'), may hold values from -6 to 6
- positions: int32 [4, 896], replicated, may hold values from 0 to 895, as said below
- plan: int32 [32, 2], P('pipe'), may hold values from 0 to 3
Outputs:
- to_next: bfloat16 [32, 896, 32, 128], P('pipe', None, 'tensor')
- to_prev: bfloat16 [32, 896, 32, 384], P('pipe', None, 'tensor')
The draws below stay inside these ranges and needn't reach their ends.
Inputs may be any that keep to these rules, and one draw needn't show every extreme that they name: `positions`: row 0 of every micro-batch starts a document; a position is 0 where a document starts and one more than the row before otherwise; one micro-batch is a single document.
All inputs are finite; a program needn't handle non-finite values.
Results may differ from the reference program's by a relative error of at most 0.0064.
Values may be sent and summed in bfloat16 or wider, within the bound.
No kernel may reach another device: no remote copies, remote signals or barrier semaphores. Data moves between devices by JAX's collectives and lax.ppermute only.
A program may use at most 64 MiB of HBM per device.

```python
import jax
import jax.numpy as jnp
from jax import lax

HD = 128
TOK = 896
MICRO = 4
HEADS = 32
SECTIONS = 32


def draw_fwd_qkv(key, part):
    key = jax.random.fold_in(key, 11)
    first = jax.random.fold_in(key, 0)
    shape = (SECTIONS, TOK, HEADS, 3 * HD)
    base = jnp.clip(jax.random.normal(first, shape, jnp.float32), -4.5, 4.5)
    return base.astype(jnp.bfloat16)


def draw_held_stash(key, part):
    key = jax.random.fold_in(key, 13)
    first = jax.random.fold_in(key, 0)
    shape = (SECTIONS, TOK, HEADS, 3 * HD)
    base = jnp.clip(jax.random.normal(first, shape, jnp.float32), -4.5, 4.5)
    return base.astype(jnp.bfloat16)


def draw_positions(key, part):
    key = jax.random.fold_in(key, 7)
    first, second = jax.random.split(key)
    rows = jnp.arange(TOK, dtype=jnp.int32)[None, :]
    batches = jnp.arange(MICRO, dtype=jnp.int32)[:, None]
    single = jax.random.randint(second, (), 0, MICRO)
    starts = jax.random.randint(first, (MICRO, TOK), 0, 160) == 0
    starts = starts & (rows % 128 != 100) & (batches != single) | (rows == 0)
    latest = lax.cummax(jnp.where(starts, rows, 0), axis=1)
    return (rows - latest).astype(jnp.int32)


def set_ends(drawn, rng, low, high):
    longest = drawn.shape.index(max(drawn.shape))
    spots = []
    for shift in (0, 1):
        where = [jax.random.randint(jax.random.fold_in(rng, axis), (), 0, length) for axis, length in enumerate(drawn.shape)]
        where[longest] = (where[longest] + shift) % drawn.shape[longest]
        spots.append(tuple(where))
    return drawn.at[spots[0]].set(low).at[spots[1]].set(high)


def level_of(rng, extent, pieces, smallest, largest):
    def one(position, shards_of):
        heights = jax.random.uniform(jax.random.fold_in(jax.random.fold_in(rng, 6), position), (shards_of,), jnp.float32, smallest / len(pieces), largest / len(pieces))
        return jnp.repeat(jnp.exp(heights), extent[position] // shards_of).reshape((-1,) + (1,) * (len(extent) - position - 1))

    loudness = one(*pieces[0])
    for cut in pieces[1:]:
        loudness = loudness * one(*cut)
    return loudness


def centred(rng, extent, scale, bound, pieces=(), held_as=jnp.bfloat16):
    entries = jax.random.normal(rng, extent, jnp.float32) * scale
    if len(pieces) > 0:
        entries = level_of(rng, extent, pieces, -0.22, 0.18) * entries
    return jnp.clip(entries, min=-bound, max=bound).astype(held_as)


def setup_inputs(seed: int = 0) -> dict:
    seeds = jax.random.split(jax.random.key(seed), 6)
    return {
        "fwd_qkv": draw_fwd_qkv(jax.random.fold_in(seeds[5], 71), 0),
        "held_stash": draw_held_stash(jax.random.fold_in(seeds[5], 71), 0),
        "d_out": centred(seeds[2], (SECTIONS, TOK, HEADS, HD), 1.0, 6.0, ((0, 32), (2, 16))),
        "positions": draw_positions(jax.random.fold_in(seeds[5], 71), 0),
        "plan": set_ends(jax.random.randint(seeds[4], (SECTIONS, 2), 0, MICRO), jax.random.fold_in(seeds[4], 1), 0, MICRO - 1).astype(jnp.int32),
    }


def visible_of(pos):
    count = pos.shape[0]
    rows = lax.broadcasted_iota(jnp.int32, (count, count), 0)
    cols = lax.broadcasted_iota(jnp.int32, (count, count), 1)
    return (cols <= rows) & (cols >= rows - pos[:, None])


def probabilities(query, keys, pos):
    scale = query.shape[-1] ** -0.5
    scores = jnp.einsum("thd,shd->hts", query.astype(jnp.float32), keys.astype(jnp.float32)) * scale
    scores = jnp.where(visible_of(pos)[None], scores, -jnp.inf)
    top = jnp.max(scores, axis=-1, keepdims=True)
    expo = jnp.exp(scores - top)
    return expo / jnp.sum(expo, axis=-1, keepdims=True)


def forward_of(packed, pos):
    width = packed.shape[-1] // 3
    query = packed[..., :width]
    keys = packed[..., width:2 * width]
    values = packed[..., 2 * width:]
    probs = probabilities(query, keys, pos)
    weights = lax.optimization_barrier(probs.astype(jnp.bfloat16)).astype(jnp.float32)
    result = jnp.einsum("hts,shd->thd", weights, values.astype(jnp.float32))
    return result.astype(jnp.bfloat16)


def backward_of(packed, pos, grad_out):
    width = packed.shape[-1] // 3
    scale = width ** -0.5
    query = packed[..., :width].astype(jnp.float32)
    keys = packed[..., width:2 * width].astype(jnp.float32)
    values = packed[..., 2 * width:].astype(jnp.float32)
    probs = probabilities(packed[..., :width], packed[..., width:2 * width], pos)
    weights = lax.optimization_barrier(probs.astype(jnp.bfloat16)).astype(jnp.float32)
    upstream = grad_out.astype(jnp.float32)
    grad_values = jnp.einsum("hts,thd->shd", weights, upstream)
    grad_probs = jnp.einsum("thd,shd->hts", upstream, values)
    delta = jnp.sum(probs * grad_probs, axis=-1, keepdims=True)
    grad_scores = (probs * (grad_probs - delta) * scale).astype(jnp.bfloat16)
    grad_scores = lax.optimization_barrier(grad_scores).astype(jnp.float32)
    grad_query = jnp.einsum("hts,shd->thd", grad_scores, keys)
    grad_keys = jnp.einsum("hts,thd->shd", grad_scores, query)
    return jnp.concatenate([grad_query.astype(jnp.bfloat16), grad_keys.astype(jnp.bfloat16), grad_values.astype(jnp.bfloat16)], axis=-1)


def reference(fwd_qkv, held_stash, d_out, positions, plan):
    sections = fwd_qkv.shape[0]

    def per_section(index):
        forward_pos = positions[plan[index, 0]]
        backward_pos = positions[plan[index, 1]]
        result = forward_of(fwd_qkv[index], forward_pos)
        grads = backward_of(held_stash[sections - 1 - index], backward_pos, d_out[index])
        return result, grads

    outputs, gradients = lax.map(per_section, jnp.arange(sections, dtype=jnp.int32))
    to_next = jnp.concatenate([jnp.zeros_like(outputs[:1]), outputs[:-1]], axis=0)
    to_prev = jnp.concatenate([gradients[1:], jnp.zeros_like(gradients[:1])], axis=0)
    return to_next, to_prev
```

```python
import jax
import jax.numpy as jnp
from jax import lax
from jax.experimental import pallas as pl
from jax.experimental.pallas import tpu as pltpu
from jax.sharding import PartitionSpec as P

GROUPS = 4
LANES = 4
BLOCK = 128


def visible_in(start, low, width, count):
    keys = lax.broadcasted_iota(jnp.int32, (count, width), 0)
    queries = lax.broadcasted_iota(jnp.int32, (count, width), 1) + low
    return (keys <= queries) & (keys >= start)


def probabilities(query, keys, start, low, scale):
    scores = lax.dot_general(
        keys, query, (((1,), (1,)), ((), ())), preferred_element_type=jnp.float32
    )
    scores = jnp.where(
        visible_in(start, low, query.shape[0], keys.shape[0]), scores * scale, -jnp.inf
    )
    top = jnp.max(scores, axis=0, keepdims=True)
    expo = jnp.exp(scores - top)
    return expo * (1.0 / jnp.sum(expo, axis=0, keepdims=True))


def document_starts(pos_ref, which):
    pos = pos_ref[pl.ds(which, 1), :]
    return lax.broadcasted_iota(jnp.int32, pos.shape, 1) - pos


def forward_kernel(which_ref, pos_ref, packed_ref, out_ref):
    heads, count, width = packed_ref.shape[0], packed_ref.shape[1], packed_ref.shape[2] // 3
    starts = document_starts(pos_ref, which_ref[0])
    for head in range(heads):
        values_t = packed_ref[head, :, 2 * width :].T
        for low in range(0, count, BLOCK):
            high = low + BLOCK
            probs = probabilities(
                packed_ref[head, low:high, :width],
                packed_ref[head, :high, width : 2 * width],
                starts[:, low:high],
                low,
                width**-0.5,
            )
            result = jnp.dot(
                values_t[:, :high], probs.astype(jnp.bfloat16), preferred_element_type=jnp.float32
            )
            out_ref[head, low:high, :] = result.T.astype(jnp.bfloat16)


def backward_kernel(
    which_ref, place_ref, pos_ref, grad_ref, early_ref, late_ref, out_ref, rows_ref, dk_ref, dv_ref
):
    heads, count, width = grad_ref.shape
    scale = width**-0.5
    starts = document_starts(pos_ref, which_ref[0])
    group, lane = place_ref[0], place_ref[1]
    piece = count // (GROUPS * LANES)
    for head in range(heads):
        for far in range(GROUPS):
            for side in range(LANES):
                source = lax.rem(group - far + GROUPS, GROUPS) * LANES + lax.rem(
                    lane - side + LANES, LANES
                )
                held = early_ref if far % 2 == 0 else late_ref
                rows_ref[pl.ds(pl.multiple_of(source * piece, 8), piece), :] = held[
                    far // 2, side, head
                ].astype(jnp.float32)
        keys_t = rows_ref[:, width : 2 * width].astype(jnp.bfloat16).T
        for low in range(0, count, BLOCK):
            high = low + BLOCK
            query = rows_ref[low:high, :width].astype(jnp.bfloat16)
            keys = rows_ref[:high, width : 2 * width].astype(jnp.bfloat16)
            values = rows_ref[:high, 2 * width :].astype(jnp.bfloat16)
            grad = grad_ref[head, low:high, :]
            probs = probabilities(query, keys, starts[:, low:high], low, scale)
            grad_probs = lax.dot_general(
                values, grad, (((1,), (1,)), ((), ())), preferred_element_type=jnp.float32
            )
            delta = jnp.sum(probs * grad_probs, axis=0, keepdims=True)
            grad_scores = (probs * (grad_probs - delta) * scale).astype(jnp.bfloat16)
            grad_values = jnp.dot(
                probs.astype(jnp.bfloat16), grad, preferred_element_type=jnp.float32
            )
            grad_keys = jnp.dot(grad_scores, query, preferred_element_type=jnp.float32)
            grad_query = jnp.dot(keys_t[:, :high], grad_scores, preferred_element_type=jnp.float32)
            out_ref[head, low:high, :width] = grad_query.T.astype(jnp.bfloat16)
            if low > 0:
                dv_ref[:low, :] += grad_values[:low]
                dk_ref[:low, :] += grad_keys[:low]
            dv_ref[low:high, :] = grad_values[low:]
            dk_ref[low:high, :] = grad_keys[low:]
        out_ref[head, :, width : 2 * width] = dk_ref[...].astype(jnp.bfloat16)
        out_ref[head, :, 2 * width :] = dv_ref[...].astype(jnp.bfloat16)


SCALARS = pl.BlockSpec(memory_space=pltpu.SMEM)
ARRAY = pl.BlockSpec(memory_space=pltpu.VMEM)
LIMIT = pltpu.CompilerParams(vmem_limit_bytes=32 * 1024 * 1024)


def forward_of(which, positions, packed):
    heads, count, width = packed.shape[0], packed.shape[1], packed.shape[2] // 3
    return pl.pallas_call(
        forward_kernel,
        out_shape=jax.ShapeDtypeStruct((heads, count, width), jnp.bfloat16),
        in_specs=[SCALARS, ARRAY, ARRAY],
        out_specs=ARRAY,
        compiler_params=LIMIT,
        name="forward_attention",
    )(which, positions, packed)


def backward_of(which, place, positions, grad_out, early, late):
    heads, count, width = grad_out.shape
    return pl.pallas_call(
        backward_kernel,
        out_shape=jax.ShapeDtypeStruct((heads, count, 3 * width), jnp.bfloat16),
        in_specs=[SCALARS, SCALARS] + [ARRAY] * 4,
        out_specs=ARRAY,
        scratch_shapes=[
            pltpu.VMEM((count, 3 * width), jnp.float32),
            pltpu.VMEM((count, width), jnp.float32),
            pltpu.VMEM((count, width), jnp.float32),
        ],
        compiler_params=LIMIT,
        name="backward_attention",
    )(which, place, positions, grad_out, early, late)


def passed_along(block, distance):
    count = lax.axis_size("pipe")
    route = [(i, i + distance) for i in range(count) if 0 <= i + distance < count]
    return lax.ppermute(block, "pipe", route)


def to_mirror(block, far):
    sections, size = lax.axis_size("pipe"), lax.axis_size("tensor")
    route = [
        (p * size + t, (sections - 2 - p) * size + (t + far * LANES) % size)
        for p in range(sections - 1)
        for t in range(size)
    ]
    return lax.ppermute(block, ("pipe", "tensor"), route)


def across_lanes(blocks):
    size = lax.axis_size("tensor")
    moved = [blocks[:, 0]]
    for side in range(1, LANES):
        route = [(t, t // LANES * LANES + (t + side) % LANES) for t in range(size)]
        moved.append(lax.ppermute(blocks[:, side], "tensor", route))
    return jnp.stack(moved, axis=1)


def local(fwd_qkv, held_stash, d_out, positions, plan):
    me = lax.axis_index("tensor")
    group, lane = me // LANES, me % LANES
    rows, heads, width = held_stash.shape[1:]
    mine = heads // (GROUPS * LANES)
    pieces = held_stash[0].transpose(1, 0, 2).reshape(GROUPS, LANES, mine, rows, width)
    pieces = jnp.roll(jnp.roll(pieces, -group, 0), -lane, 1)

    first = jnp.stack([to_mirror(pieces[0], 0), to_mirror(pieces[2], 2)])
    crossed = across_lanes(jnp.stack([pieces[1], pieces[3]]))
    late = jnp.stack([to_mirror(crossed[0], 1), to_mirror(crossed[1], 3)])
    early = across_lanes(first)

    attn_out = forward_of(plan[0, :1], positions, fwd_qkv[0].transpose(1, 0, 2))
    to_next = passed_along(attn_out, 1).transpose(1, 0, 2)

    grad_out = passed_along(d_out[0].transpose(1, 0, 2), -1)
    which = passed_along(plan, -1)
    place = jnp.stack([group, lane]).astype(jnp.int32)
    grads = backward_of(which[0, 1:], place, positions, grad_out, early, late)
    return to_next[None], grads.transpose(1, 0, 2)[None]


def solution(mesh):
    placed = (
        P("pipe", None, "tensor", None),
        P("pipe", "tensor", None, None),
        P("pipe", None, "tensor", None),
        P(),
        P("pipe", None),
    )
    return jax.shard_map(
        local,
        mesh=mesh,
        in_specs=placed,
        out_specs=(P("pipe", None, "tensor", None), P("pipe", None, "tensor", None)),
        check_vma=False,
    )
```

```python
import functools

import jax
import jax.numpy as jnp
from jax import lax
from jax.experimental import pallas as pl
from jax.experimental.pallas import tpu as pltpu
from jax.sharding import PartitionSpec as P

GROUPS = 4
LANES = 4
BLOCK = 128
FLOPS = 50_000_000_000
FIRST = (0, 2, )
LATE = (1, 3, )


def visible_in(start, low, width, count):
    keys = lax.broadcasted_iota(jnp.int32, (count, width), 0)
    queries = lax.broadcasted_iota(jnp.int32, (count, width), 1) + low
    return (keys <= queries) & (keys >= start)


def probabilities(query, keys, start, low, scale):
    scores = lax.dot_general(
        keys, query, (((1,), (1,)), ((), ())), preferred_element_type=jnp.float32
    )
    scores = jnp.where(
        visible_in(start, low, query.shape[0], keys.shape[0]), scores * scale, -jnp.inf
    )
    top = jnp.max(scores, axis=0, keepdims=True)
    expo = jnp.exp(scores - top)
    return expo * (1.0 / jnp.sum(expo, axis=0, keepdims=True))


def document_starts(pos_ref, which, low, width):
    starts = jnp.zeros((1, width), jnp.int32)
    for batch in range(pos_ref.shape[0]):
        starts = jnp.where(which == batch, pos_ref[batch : batch + 1, low : low + width], starts)
    return lax.broadcasted_iota(jnp.int32, starts.shape, 1) + low - starts


def forward_kernel(head, which_ref, pos_ref, packed_ref, out_ref):
    count, width = packed_ref.shape[1], packed_ref.shape[2] // 3
    values_t = packed_ref[head, :, 2 * width :].T
    for low in range(0, count, BLOCK):
        high = low + BLOCK
        probs = probabilities(
            packed_ref[head, low:high, :width],
            packed_ref[head, :high, width : 2 * width],
            document_starts(pos_ref, which_ref[0, 0], low, BLOCK),
            low,
            width**-0.5,
        )
        result = jnp.dot(
            values_t[:, :high], probs.astype(jnp.bfloat16), preferred_element_type=jnp.float32
        )
        out_ref[low:high, :] = result.T.astype(jnp.bfloat16)


def backward_kernel(
    place_ref, pos_ref, grad_ref, early_ref, late_ref, out_ref, rows_ref, dk_ref, dv_ref
):
    heads, count, width = out_ref.shape[0], out_ref.shape[1], grad_ref.shape[2]
    scale = width**-0.5
    which = grad_ref[0, count : count + 1, :].astype(jnp.float32)
    group = place_ref[0]
    piece = count // (GROUPS * LANES)
    for head in range(heads):
        for far in range(GROUPS):
            for side in range(LANES):
                source = lax.rem(group - far + GROUPS, GROUPS) * LANES + side
                held, number = (early_ref, FIRST.index(far)) if far in FIRST else (late_ref, LATE.index(far))
                rows_ref[pl.ds(pl.multiple_of(source * piece, 8), piece), :] = held[
                    number, side, head
                ].astype(jnp.float32)
        keys_t = rows_ref[:, width : 2 * width].astype(jnp.bfloat16).T
        for low in range(0, count, BLOCK):
            high = low + BLOCK
            query = rows_ref[low:high, :width].astype(jnp.bfloat16)
            keys = rows_ref[:high, width : 2 * width].astype(jnp.bfloat16)
            values = rows_ref[:high, 2 * width :].astype(jnp.bfloat16)
            grad = grad_ref[head, low:high, :]
            starts = document_starts(pos_ref, which, low, BLOCK)
            probs = probabilities(query, keys, starts, low, scale)
            grad_probs = lax.dot_general(
                values, grad, (((1,), (1,)), ((), ())), preferred_element_type=jnp.float32
            )
            delta = jnp.sum(probs * grad_probs, axis=0, keepdims=True)
            grad_scores = (probs * (grad_probs - delta) * scale).astype(jnp.bfloat16)
            grad_values = jnp.dot(
                probs.astype(jnp.bfloat16), grad, preferred_element_type=jnp.float32
            )
            grad_keys = jnp.dot(grad_scores, query, preferred_element_type=jnp.float32)
            grad_query = jnp.dot(keys_t[:, :high], grad_scores, preferred_element_type=jnp.float32)
            out_ref[head, low:high, :width] = grad_query.T.astype(jnp.bfloat16)
            if low > 0:
                dv_ref[:low, :] += grad_values[:low]
                dk_ref[:low, :] += grad_keys[:low]
            dv_ref[low:high, :] = grad_values[low:]
            dk_ref[low:high, :] = grad_keys[low:]
        out_ref[head, :, width : 2 * width] = dk_ref[...].astype(jnp.bfloat16)
        out_ref[head, :, 2 * width :] = dv_ref[...].astype(jnp.bfloat16)


SCALARS = pl.BlockSpec(memory_space=pltpu.SMEM)
ARRAY = pl.BlockSpec(memory_space=pltpu.VMEM)
LIMIT = pltpu.CompilerParams(vmem_limit_bytes=32 * 1024 * 1024)


def forward_of(head, plan, positions, packed):
    count, width = packed.shape[1], packed.shape[2] // 3
    return pl.pallas_call(
        functools.partial(forward_kernel, head),
        out_shape=jax.ShapeDtypeStruct((count, width), jnp.bfloat16),
        in_specs=[SCALARS, ARRAY, ARRAY],
        out_specs=ARRAY,
        compiler_params=LIMIT,
        cost_estimate=pl.CostEstimate(flops=FLOPS, bytes_accessed=0, transcendentals=0),
        name="forward_attention",
    )(plan, positions, packed)


def backward_of(place, positions, grad_out, early, late):
    width = grad_out.shape[2]
    heads, count = early.shape[2], positions.shape[1]
    return pl.pallas_call(
        backward_kernel,
        out_shape=jax.ShapeDtypeStruct((heads, count, 3 * width), jnp.bfloat16),
        in_specs=[SCALARS] + [ARRAY] * 4,
        out_specs=ARRAY,
        scratch_shapes=[
            pltpu.VMEM((count, 3 * width), jnp.float32),
            pltpu.VMEM((count, width), jnp.float32),
            pltpu.VMEM((count, width), jnp.float32),
        ],
        compiler_params=LIMIT,
        name="backward_attention",
    )(place, positions, grad_out, early, late)


def stack_kernel(*refs):
    for number, ref in enumerate(refs[:-1]):
        refs[-1][number] = ref[...]


def stacked(pieces):
    return pl.pallas_call(
        stack_kernel,
        out_shape=jax.ShapeDtypeStruct((len(pieces), *pieces[0].shape), pieces[0].dtype),
        in_specs=[ARRAY] * len(pieces),
        out_specs=ARRAY,
        compiler_params=LIMIT,
        cost_estimate=pl.CostEstimate(flops=FLOPS, bytes_accessed=0, transcendentals=0),
        name="stacked",
    )(*pieces)


def passed_along(block, distance):
    count = lax.axis_size("pipe")
    route = [(i, i + distance) for i in range(count) if 0 <= i + distance < count]
    return lax.ppermute(block, "pipe", route)


def to_mirror(block, far):
    sections, size = lax.axis_size("pipe"), lax.axis_size("tensor")
    route = [
        (p * size + t, (sections - 2 - p) * size + (t + far * LANES) % size)
        for p in range(sections - 1)
        for t in range(size)
    ]
    return lax.ppermute(block, ("pipe", "tensor"), route)


def across_lanes(blocks):
    size = lax.axis_size("tensor")
    rows = [list(range(low, low + LANES)) for low in range(0, size, LANES)]
    return lax.all_to_all(
        blocks, "tensor", split_axis=1, concat_axis=1, axis_index_groups=rows, tiled=True
    )


def local(fwd_qkv, held_stash, d_out, positions, plan):
    me = lax.axis_index("tensor")
    group = me // LANES
    rows, heads, width = held_stash.shape[1:]
    mine = heads // (GROUPS * LANES)
    count = d_out.shape[1]

    def for_group(far):
        low = (group + far) % GROUPS * (LANES * mine)
        piece = lax.dynamic_slice_in_dim(held_stash[0], low, LANES * mine, 1)
        return piece.reshape(rows * LANES * mine, width)

    def by_lane(pieces):
        split = pieces.reshape(-1, rows, LANES, mine, width).transpose(0, 2, 3, 1, 4)
        return split

    def after(value, other):
        return lax.optimization_barrier((value, other))[0]

    first = stacked([to_mirror(for_group(far), far) for far in FIRST])
    crossed = across_lanes(by_lane(jnp.stack([for_group(far) for far in LATE])))
    late = stacked([to_mirror(crossed[n], far) for n, far in enumerate(LATE)])
    early = across_lanes(by_lane(first))
    packed = fwd_qkv[0].transpose(1, 0, 2)
    attn_out = jnp.stack([forward_of(head, plan, positions, packed) for head in range(mine)])
    which = jnp.broadcast_to(plan[0, 1].astype(jnp.bfloat16), (mine, 16, d_out.shape[3]))
    grad_out = passed_along(jnp.concatenate([after(d_out, attn_out)[0].transpose(1, 0, 2), which], axis=1), -1)
    to_next = passed_along(after(attn_out, grad_out), 1).transpose(1, 0, 2)
    place = group.astype(jnp.int32)[None]
    grads = backward_of(place, positions, grad_out, early, late)
    return to_next[None], grads.transpose(1, 0, 2)[None]


def solution(mesh):
    placed = (
        P("pipe", None, "tensor", None),
        P("pipe", "tensor", None, None),
        P("pipe", None, "tensor", None),
        P(),
        P("pipe", None),
    )
    return jax.shard_map(
        local,
        mesh=mesh,
        in_specs=placed,
        out_specs=(P("pipe", None, "tensor", None), P("pipe", None, "tensor", None)),
        check_vma=False,
    )
```

```python
import functools

import jax
import jax.numpy as jnp
from jax import lax
from jax.experimental import pallas as pl
from jax.experimental.pallas import tpu as pltpu
from jax.sharding import PartitionSpec as P

GROUPS = 4
LANES = 4
BLOCK = 128
WIDE = 256
FLOPS = 50_000_000_000
FIRST = (0, 2, )
LATE = (1, 3, )


def visible_in(start, low, width, count):
    keys = lax.broadcasted_iota(jnp.int32, (count, width), 0)
    queries = lax.broadcasted_iota(jnp.int32, (count, width), 1) + low
    return (keys <= queries) & (keys >= start)


def probabilities(query, keys, start, low, scale):
    scores = lax.dot_general(
        keys, query, (((1,), (1,)), ((), ())), preferred_element_type=jnp.float32
    )
    scores = jnp.where(
        visible_in(start, low, query.shape[0], keys.shape[0]), scores * scale, -jnp.inf
    )
    top = jnp.max(scores, axis=0, keepdims=True)
    expo = jnp.exp(scores - top)
    return expo * (1.0 / jnp.sum(expo, axis=0, keepdims=True))


def document_starts(pos_ref, which, low, width):
    starts = jnp.zeros((1, width), jnp.int32)
    for batch in range(pos_ref.shape[0]):
        starts = jnp.where(which == batch, pos_ref[batch : batch + 1, low : low + width], starts)
    return lax.broadcasted_iota(jnp.int32, starts.shape, 1) + low - starts


def forward_kernel(head, which_ref, pos_ref, packed_ref, out_ref):
    count, width = packed_ref.shape[1], packed_ref.shape[2] // 3
    values_t = packed_ref[head, :, 2 * width :].T
    for low in range(0, count, BLOCK):
        high = low + BLOCK
        probs = probabilities(
            packed_ref[head, low:high, :width],
            packed_ref[head, :high, width : 2 * width],
            document_starts(pos_ref, which_ref[0, 0], low, BLOCK),
            low,
            width**-0.5,
        )
        result = jnp.dot(
            values_t[:, :high], probs.astype(jnp.bfloat16), preferred_element_type=jnp.float32
        )
        out_ref[low:high, :] = result.T.astype(jnp.bfloat16)


def backward_kernel(
    place_ref, pos_ref, grad_ref, early_ref, late_ref, out_ref, rows_ref, probs_ref, scores_ref
):
    heads, count, width = out_ref.shape[0], out_ref.shape[1], grad_ref.shape[2]
    scale = width**-0.5
    which = grad_ref[0, count : count + 1, :1].astype(jnp.float32)
    group = place_ref[0]
    piece = count // (GROUPS * LANES)
    for far in range(GROUPS):
        held, number = (early_ref, FIRST.index(far)) if far in FIRST else (late_ref, LATE.index(far))
        source = lax.rem(group - far + GROUPS, GROUPS) * LANES
        for side in range(0, LANES, 2):
            place = pl.ds(pl.multiple_of((source + side) * piece, 2 * piece), 2 * piece)
            for head in range(heads):
                both = [held[number, side + n, head].astype(jnp.float32) for n in range(2)]
                rows_ref[head, place, :] = jnp.concatenate(both).astype(jnp.bfloat16)
    keys_t = [rows_ref[head, :, width : 2 * width].T for head in range(heads)]
    for low in range(0, count, WIDE):
        high = min(low + WIDE, count)
        starts = document_starts(pos_ref, which, low, high - low)
        for head in range(heads):
            query = rows_ref[head, low:high, :width]
            keys = rows_ref[head, :high, width : 2 * width]
            values = rows_ref[head, :high, 2 * width :]
            probs = probabilities(query, keys, starts, low, scale)
            grad_probs = lax.dot_general(
                values,
                grad_ref[head, low:high, :],
                (((1,), (1,)), ((), ())),
                preferred_element_type=jnp.float32,
            )
            delta = jnp.sum(probs * grad_probs, axis=0, keepdims=True)
            grad_scores = (probs * (grad_probs - delta) * scale).astype(jnp.bfloat16)
            probs_ref[head, :high, low:high] = probs.astype(jnp.bfloat16)
            scores_ref[head, :high, low:high] = grad_scores
            grad_query = jnp.dot(
                keys_t[head][:, :high], grad_scores, preferred_element_type=jnp.float32
            )
            out_ref[head, low:high, :width] = grad_query.T.astype(jnp.bfloat16)
    for low in range(0, count, WIDE):
        high = min(low + WIDE, count)
        for head in range(heads):
            out_ref[head, low:high, width : 2 * width] = jnp.dot(
                scores_ref[head, low:high, low:],
                rows_ref[head, low:, :width],
                preferred_element_type=jnp.float32,
            ).astype(jnp.bfloat16)
            out_ref[head, low:high, 2 * width :] = jnp.dot(
                probs_ref[head, low:high, low:],
                grad_ref[head, low:count, :],
                preferred_element_type=jnp.float32,
            ).astype(jnp.bfloat16)


SCALARS = pl.BlockSpec(memory_space=pltpu.SMEM)
ARRAY = pl.BlockSpec(memory_space=pltpu.VMEM)
LIMIT = pltpu.CompilerParams(vmem_limit_bytes=32 * 1024 * 1024)


def forward_of(head, plan, positions, packed):
    count, width = packed.shape[1], packed.shape[2] // 3
    return pl.pallas_call(
        functools.partial(forward_kernel, head),
        out_shape=jax.ShapeDtypeStruct((count, width), jnp.bfloat16),
        in_specs=[SCALARS, ARRAY, ARRAY],
        out_specs=ARRAY,
        compiler_params=LIMIT,
        cost_estimate=pl.CostEstimate(flops=FLOPS, bytes_accessed=0, transcendentals=0),
        name="forward_attention",
    )(plan, positions, packed)


def backward_of(place, positions, grad_out, early, late):
    width = grad_out.shape[2]
    heads, count = early.shape[2], positions.shape[1]
    return pl.pallas_call(
        backward_kernel,
        out_shape=jax.ShapeDtypeStruct((heads, count, 3 * width), jnp.bfloat16),
        in_specs=[SCALARS] + [ARRAY] * 4,
        out_specs=ARRAY,
        scratch_shapes=[
            pltpu.VMEM((heads, count, 3 * width), jnp.bfloat16),
            pltpu.VMEM((heads, count, count), jnp.bfloat16),
            pltpu.VMEM((heads, count, count), jnp.bfloat16),
        ],
        compiler_params=LIMIT,
        name="backward_attention",
    )(place, positions, grad_out, early, late)


def stack_kernel(*refs):
    for number, ref in enumerate(refs[:-1]):
        refs[-1][number] = ref[...]


def stacked(pieces):
    return pl.pallas_call(
        stack_kernel,
        out_shape=jax.ShapeDtypeStruct((len(pieces), *pieces[0].shape), pieces[0].dtype),
        in_specs=[ARRAY] * len(pieces),
        out_specs=ARRAY,
        compiler_params=LIMIT,
        cost_estimate=pl.CostEstimate(flops=FLOPS, bytes_accessed=0, transcendentals=0),
        name="stacked",
    )(*pieces)


def passed_along(block, distance):
    count = lax.axis_size("pipe")
    route = [(i, i + distance) for i in range(count) if 0 <= i + distance < count]
    return lax.ppermute(block, "pipe", route)


def to_mirror(block, far):
    sections, size = lax.axis_size("pipe"), lax.axis_size("tensor")
    route = [
        (p * size + t, (sections - 2 - p) * size + (t + far * LANES) % size)
        for p in range(sections - 1)
        for t in range(size)
    ]
    return lax.ppermute(block, ("pipe", "tensor"), route)


def across_lanes(blocks):
    size = lax.axis_size("tensor")
    rows = [list(range(low, low + LANES)) for low in range(0, size, LANES)]
    return lax.all_to_all(
        blocks, "tensor", split_axis=1, concat_axis=1, axis_index_groups=rows, tiled=True
    )


def local(fwd_qkv, held_stash, d_out, positions, plan):
    me = lax.axis_index("tensor")
    group = me // LANES
    rows, heads, width = held_stash.shape[1:]
    mine = heads // (GROUPS * LANES)
    count = d_out.shape[1]

    def for_group(far):
        low = (group + far) % GROUPS * (LANES * mine)
        piece = lax.dynamic_slice_in_dim(held_stash[0], low, LANES * mine, 1)
        return piece.reshape(rows * LANES * mine, width)

    def by_lane(pieces):
        split = pieces.reshape(-1, rows, LANES, mine, width).transpose(0, 2, 3, 1, 4)
        return split

    def after(value, other):
        return lax.optimization_barrier((value, other))[0]

    first = stacked([to_mirror(for_group(far), far) for far in FIRST])
    crossed = across_lanes(by_lane(jnp.stack([for_group(far) for far in LATE])))
    late = stacked([to_mirror(crossed[n], far) for n, far in enumerate(LATE)])
    early = across_lanes(by_lane(first))
    packed = fwd_qkv[0].transpose(1, 0, 2)
    attn_out = jnp.stack([forward_of(head, plan, positions, packed) for head in range(mine)])
    which = jnp.broadcast_to(plan[0, 1].astype(jnp.bfloat16), (mine, 16, d_out.shape[3]))
    grad_out = passed_along(jnp.concatenate([after(d_out, attn_out)[0].transpose(1, 0, 2), which], axis=1), -1)
    to_next = passed_along(after(attn_out, grad_out), 1).transpose(1, 0, 2)
    place = group.astype(jnp.int32)[None]
    grads = backward_of(place, positions, grad_out, early, late)
    return to_next[None], grads.transpose(1, 0, 2)[None]


def solution(mesh):
    placed = (
        P("pipe", None, "tensor", None),
        P("pipe", "tensor", None, None),
        P("pipe", None, "tensor", None),
        P(),
        P("pipe", None),
    )
    return jax.shard_map(
        local,
        mesh=mesh,
        in_specs=placed,
        out_specs=(P("pipe", None, "tensor", None), P("pipe", None, "tensor", None)),
        check_vma=False,
    )
```

```python
import functools

import jax
import jax.numpy as jnp
from jax import lax
from jax.experimental import pallas as pl
from jax.experimental.pallas import tpu as pltpu
from jax.sharding import PartitionSpec as P

GROUPS = 4
LANES = 4
BLOCK = 128
WIDE = 256
FLOPS = 50_000_000_000
FIRST = (2, 0)
LATE = (1, 3, )


def visible_in(start, low, width, count):
    keys = lax.broadcasted_iota(jnp.int32, (count, width), 0)
    queries = lax.broadcasted_iota(jnp.int32, (count, width), 1) + low
    return (keys <= queries) & (keys >= start)


def probabilities(query, keys, start, low, scale):
    scores = lax.dot_general(
        keys, query, (((1,), (1,)), ((), ())), preferred_element_type=jnp.float32
    )
    scores = jnp.where(
        visible_in(start, low, query.shape[0], keys.shape[0]), scores * scale, -jnp.inf
    )
    top = jnp.max(scores, axis=0, keepdims=True)
    expo = jnp.exp(scores - top)
    return expo * (1.0 / jnp.sum(expo, axis=0, keepdims=True))


def document_starts(pos_ref, which, low, width):
    starts = jnp.zeros((1, width), jnp.int32)
    for batch in range(pos_ref.shape[0]):
        starts = jnp.where(which == batch, pos_ref[batch : batch + 1, low : low + width], starts)
    return lax.broadcasted_iota(jnp.int32, starts.shape, 1) + low - starts


def forward_kernel(head, which_ref, pos_ref, packed_ref, out_ref):
    count, width = packed_ref.shape[1], packed_ref.shape[2] // 3
    values_t = packed_ref[head, :, 2 * width :].T
    for low in range(0, count, BLOCK):
        high = low + BLOCK
        probs = probabilities(
            packed_ref[head, low:high, :width],
            packed_ref[head, :high, width : 2 * width],
            document_starts(pos_ref, which_ref[0, 0], low, BLOCK),
            low,
            width**-0.5,
        )
        result = jnp.dot(
            values_t[:, :high], probs.astype(jnp.bfloat16), preferred_element_type=jnp.float32
        )
        out_ref[low:high, :] = result.T.astype(jnp.bfloat16)


def backward_kernel(
    place_ref, pos_ref, grad_ref, early_ref, late_ref, out_ref, rows_ref, probs_ref, scores_ref
):
    heads, count, width = out_ref.shape[0], out_ref.shape[1], grad_ref.shape[2]
    scale = width**-0.5
    which = grad_ref[0, count : count + 1, :1].astype(jnp.float32)
    group = place_ref[0]
    piece = count // (GROUPS * LANES)
    for far in range(GROUPS):
        held, number = (early_ref, FIRST.index(far)) if far in FIRST else (late_ref, LATE.index(far))
        source = lax.rem(group - far + GROUPS, GROUPS) * LANES
        for side in range(0, LANES, 2):
            place = pl.ds(pl.multiple_of((source + side) * piece, 2 * piece), 2 * piece)
            for head in range(heads):
                both = [held[number, side + n, head].astype(jnp.float32) for n in range(2)]
                rows_ref[head, place, :] = jnp.concatenate(both).astype(jnp.bfloat16)
    keys_t = [rows_ref[head, :, width : 2 * width].T for head in range(heads)]
    for low in range(0, count, WIDE):
        high = min(low + WIDE, count)
        starts = document_starts(pos_ref, which, low, high - low)
        for head in range(heads):
            query = rows_ref[head, low:high, :width]
            keys = rows_ref[head, :high, width : 2 * width]
            values = rows_ref[head, :high, 2 * width :]
            probs = probabilities(query, keys, starts, low, scale)
            grad_probs = lax.dot_general(
                values,
                grad_ref[head, low:high, :],
                (((1,), (1,)), ((), ())),
                preferred_element_type=jnp.float32,
            )
            delta = jnp.sum(probs * grad_probs, axis=0, keepdims=True)
            grad_scores = (probs * (grad_probs - delta) * scale).astype(jnp.bfloat16)
            probs_ref[head, :high, low:high] = probs.astype(jnp.bfloat16)
            scores_ref[head, :high, low:high] = grad_scores
            grad_query = jnp.dot(
                keys_t[head][:, :high], grad_scores, preferred_element_type=jnp.float32
            )
            out_ref[head, low:high, :width] = grad_query.T.astype(jnp.bfloat16)
    for low in range(0, count, WIDE):
        high = min(low + WIDE, count)
        for head in range(heads):
            out_ref[head, low:high, width : 2 * width] = jnp.dot(
                scores_ref[head, low:high, low:],
                rows_ref[head, low:, :width],
                preferred_element_type=jnp.float32,
            ).astype(jnp.bfloat16)
            out_ref[head, low:high, 2 * width :] = jnp.dot(
                probs_ref[head, low:high, low:],
                grad_ref[head, low:count, :],
                preferred_element_type=jnp.float32,
            ).astype(jnp.bfloat16)


SCALARS = pl.BlockSpec(memory_space=pltpu.SMEM)
ARRAY = pl.BlockSpec(memory_space=pltpu.VMEM)
LIMIT = pltpu.CompilerParams(vmem_limit_bytes=32 * 1024 * 1024)


def forward_of(head, plan, positions, packed):
    count, width = packed.shape[1], packed.shape[2] // 3
    return pl.pallas_call(
        functools.partial(forward_kernel, head),
        out_shape=jax.ShapeDtypeStruct((count, width), jnp.bfloat16),
        in_specs=[SCALARS, ARRAY, ARRAY],
        out_specs=ARRAY,
        compiler_params=LIMIT,
        cost_estimate=pl.CostEstimate(flops=FLOPS, bytes_accessed=0, transcendentals=0),
        name="forward_attention",
    )(plan, positions, packed)


def backward_of(place, positions, grad_out, early, late):
    width = grad_out.shape[2]
    heads, count = early.shape[2], positions.shape[1]
    return pl.pallas_call(
        backward_kernel,
        out_shape=jax.ShapeDtypeStruct((heads, count, 3 * width), jnp.bfloat16),
        in_specs=[SCALARS] + [ARRAY] * 4,
        out_specs=ARRAY,
        scratch_shapes=[
            pltpu.VMEM((heads, count, 3 * width), jnp.bfloat16),
            pltpu.VMEM((heads, count, count), jnp.bfloat16),
            pltpu.VMEM((heads, count, count), jnp.bfloat16),
        ],
        compiler_params=LIMIT,
        name="backward_attention",
    )(place, positions, grad_out, early, late)


def stack_kernel(*refs):
    for number, ref in enumerate(refs[:-1]):
        refs[-1][number] = ref[...]


def stacked(pieces):
    return pl.pallas_call(
        stack_kernel,
        out_shape=jax.ShapeDtypeStruct((len(pieces), *pieces[0].shape), pieces[0].dtype),
        in_specs=[ARRAY] * len(pieces),
        out_specs=ARRAY,
        compiler_params=LIMIT,
        cost_estimate=pl.CostEstimate(flops=FLOPS, bytes_accessed=0, transcendentals=0),
        name="stacked",
    )(*pieces)


def passed_along(block, distance):
    count = lax.axis_size("pipe")
    route = [(i, i + distance) for i in range(count) if 0 <= i + distance < count]
    return lax.ppermute(block, "pipe", route)


def to_mirror(block, far):
    sections, size = lax.axis_size("pipe"), lax.axis_size("tensor")
    route = [
        (p * size + t, (sections - 2 - p) * size + (t + far * LANES) % size)
        for p in range(sections - 1)
        for t in range(size)
    ]
    return lax.ppermute(block, ("pipe", "tensor"), route)


def across_lanes(blocks):
    size = lax.axis_size("tensor")
    rows = [list(range(low, low + LANES)) for low in range(0, size, LANES)]
    return lax.all_to_all(
        blocks, "tensor", split_axis=1, concat_axis=1, axis_index_groups=rows, tiled=True
    )


def local(fwd_qkv, held_stash, d_out, positions, plan):
    me = lax.axis_index("tensor")
    group = me // LANES
    rows, heads, width = held_stash.shape[1:]
    mine = heads // (GROUPS * LANES)
    count = d_out.shape[1]

    def for_group(far):
        low = (group + far) % GROUPS * (LANES * mine)
        piece = lax.dynamic_slice_in_dim(held_stash[0], low, LANES * mine, 1)
        return piece.reshape(rows * LANES * mine, width)

    def by_lane(pieces):
        split = pieces.reshape(-1, rows, LANES, mine, width).transpose(0, 2, 3, 1, 4)
        return split

    def after(value, other):
        return lax.optimization_barrier((value, other))[0]

    first = stacked([to_mirror(for_group(far), far) for far in FIRST])
    crossed = across_lanes(by_lane(jnp.stack([for_group(far) for far in LATE])))
    late = stacked([to_mirror(crossed[n], far) for n, far in enumerate(LATE)])
    early = across_lanes(by_lane(first))
    packed = fwd_qkv[0].transpose(1, 0, 2)
    attn_out = jnp.stack([forward_of(head, plan, positions, packed) for head in range(mine)])
    which = jnp.broadcast_to(plan[0, 1].astype(jnp.bfloat16), (mine, 16, d_out.shape[3]))
    grad_out = passed_along(jnp.concatenate([after(d_out, attn_out)[0].transpose(1, 0, 2), which], axis=1), -1)
    to_next = passed_along(after(attn_out, first), 1)
    place = group.astype(jnp.int32)[None]
    grads = backward_of(place, positions, grad_out, early, late)
    to_next = after(to_next, grads).transpose(1, 0, 2)
    return to_next[None], grads.transpose(1, 0, 2)[None]


def solution(mesh):
    placed = (
        P("pipe", None, "tensor", None),
        P("pipe", "tensor", None, None),
        P("pipe", None, "tensor", None),
        P(),
        P("pipe", None),
    )
    return jax.shard_map(
        local,
        mesh=mesh,
        in_specs=placed,
        out_specs=(P("pipe", None, "tensor", None), P("pipe", None, "tensor", None)),
        check_vma=False,
    )
```

```python
import functools

import jax
import jax.numpy as jnp
from jax import lax
from jax.experimental import pallas as pl
from jax.experimental.pallas import tpu as pltpu
from jax.sharding import PartitionSpec as P

GROUPS = 4
LANES = 4
BLOCK = 128
WIDE = 256
FLOPS = 50_000_000_000
FIRST = (0, 2, )
LATE = (3, 1)


def visible_in(start, low, width, count):
    keys = lax.broadcasted_iota(jnp.int32, (count, width), 0)
    queries = lax.broadcasted_iota(jnp.int32, (count, width), 1) + low
    return (keys <= queries) & (keys >= start)


def probabilities(query, keys, start, low, scale):
    scores = lax.dot_general(
        keys, query, (((1,), (1,)), ((), ())), preferred_element_type=jnp.float32
    )
    scores = jnp.where(
        visible_in(start, low, query.shape[0], keys.shape[0]), scores * scale, -jnp.inf
    )
    top = jnp.max(scores, axis=0, keepdims=True)
    expo = jnp.exp(scores - top)
    return expo * (1.0 / jnp.sum(expo, axis=0, keepdims=True))


def document_starts(pos_ref, which, low, width):
    starts = jnp.zeros((1, width), jnp.int32)
    for batch in range(pos_ref.shape[0]):
        starts = jnp.where(which == batch, pos_ref[batch : batch + 1, low : low + width], starts)
    return lax.broadcasted_iota(jnp.int32, starts.shape, 1) + low - starts


def forward_kernel(head, which_ref, pos_ref, packed_ref, out_ref):
    count, width = packed_ref.shape[1], packed_ref.shape[2] // 3
    values_t = packed_ref[head, :, 2 * width :].T
    for low in range(0, count, BLOCK):
        high = low + BLOCK
        probs = probabilities(
            packed_ref[head, low:high, :width],
            packed_ref[head, :high, width : 2 * width],
            document_starts(pos_ref, which_ref[0, 0], low, BLOCK),
            low,
            width**-0.5,
        )
        result = jnp.dot(
            values_t[:, :high], probs.astype(jnp.bfloat16), preferred_element_type=jnp.float32
        )
        out_ref[low:high, :] = result.T.astype(jnp.bfloat16)


def backward_kernel(
    place_ref, pos_ref, grad_ref, early_ref, late_ref, out_ref, rows_ref, probs_ref, scores_ref
):
    heads, count, width = out_ref.shape[0], out_ref.shape[1], grad_ref.shape[2]
    scale = width**-0.5
    which = grad_ref[0, count : count + 1, :1].astype(jnp.float32)
    group = place_ref[0]
    piece = count // (GROUPS * LANES)
    for far in range(GROUPS):
        held, number = (early_ref, FIRST.index(far)) if far in FIRST else (late_ref, LATE.index(far))
        source = lax.rem(group - far + GROUPS, GROUPS) * LANES
        for side in range(0, LANES, 2):
            place = pl.ds(pl.multiple_of((source + side) * piece, 2 * piece), 2 * piece)
            for head in range(heads):
                both = [held[number, side + n, head].astype(jnp.float32) for n in range(2)]
                rows_ref[head, place, :] = jnp.concatenate(both).astype(jnp.bfloat16)
    keys_t = [rows_ref[head, :, width : 2 * width].T for head in range(heads)]
    for low in range(0, count, WIDE):
        high = min(low + WIDE, count)
        starts = document_starts(pos_ref, which, low, high - low)
        for head in range(heads):
            query = rows_ref[head, low:high, :width]
            keys = rows_ref[head, :high, width : 2 * width]
            values = rows_ref[head, :high, 2 * width :]
            probs = probabilities(query, keys, starts, low, scale)
            grad_probs = lax.dot_general(
                values,
                grad_ref[head, low:high, :],
                (((1,), (1,)), ((), ())),
                preferred_element_type=jnp.float32,
            )
            delta = jnp.sum(probs * grad_probs, axis=0, keepdims=True)
            grad_scores = (probs * (grad_probs - delta) * scale).astype(jnp.bfloat16)
            probs_ref[head, :high, low:high] = probs.astype(jnp.bfloat16)
            scores_ref[head, :high, low:high] = grad_scores
            grad_query = jnp.dot(
                keys_t[head][:, :high], grad_scores, preferred_element_type=jnp.float32
            )
            out_ref[head, low:high, :width] = grad_query.T.astype(jnp.bfloat16)
    for low in range(0, count, WIDE):
        high = min(low + WIDE, count)
        for head in range(heads):
            out_ref[head, low:high, width : 2 * width] = jnp.dot(
                scores_ref[head, low:high, low:],
                rows_ref[head, low:, :width],
                preferred_element_type=jnp.float32,
            ).astype(jnp.bfloat16)
            out_ref[head, low:high, 2 * width :] = jnp.dot(
                probs_ref[head, low:high, low:],
                grad_ref[head, low:count, :],
                preferred_element_type=jnp.float32,
            ).astype(jnp.bfloat16)


SCALARS = pl.BlockSpec(memory_space=pltpu.SMEM)
ARRAY = pl.BlockSpec(memory_space=pltpu.VMEM)
LIMIT = pltpu.CompilerParams(vmem_limit_bytes=32 * 1024 * 1024)


def forward_of(head, plan, positions, packed):
    count, width = packed.shape[1], packed.shape[2] // 3
    return pl.pallas_call(
        functools.partial(forward_kernel, head),
        out_shape=jax.ShapeDtypeStruct((count, width), jnp.bfloat16),
        in_specs=[SCALARS, ARRAY, ARRAY],
        out_specs=ARRAY,
        compiler_params=LIMIT,
        cost_estimate=pl.CostEstimate(flops=FLOPS, bytes_accessed=0, transcendentals=0),
        name="forward_attention",
    )(plan, positions, packed)


def backward_of(place, positions, grad_out, early, late):
    width = grad_out.shape[2]
    heads, count = early.shape[2], positions.shape[1]
    return pl.pallas_call(
        backward_kernel,
        out_shape=jax.ShapeDtypeStruct((heads, count, 3 * width), jnp.bfloat16),
        in_specs=[SCALARS] + [ARRAY] * 4,
        out_specs=ARRAY,
        scratch_shapes=[
            pltpu.VMEM((heads, count, 3 * width), jnp.bfloat16),
            pltpu.VMEM((heads, count, count), jnp.bfloat16),
            pltpu.VMEM((heads, count, count), jnp.bfloat16),
        ],
        compiler_params=LIMIT,
        name="backward_attention",
    )(place, positions, grad_out, early, late)


def stack_kernel(*refs):
    for number, ref in enumerate(refs[:-1]):
        refs[-1][number] = ref[...]


def stacked(pieces):
    return pl.pallas_call(
        stack_kernel,
        out_shape=jax.ShapeDtypeStruct((len(pieces), *pieces[0].shape), pieces[0].dtype),
        in_specs=[ARRAY] * len(pieces),
        out_specs=ARRAY,
        compiler_params=LIMIT,
        cost_estimate=pl.CostEstimate(flops=FLOPS, bytes_accessed=0, transcendentals=0),
        name="stacked",
    )(*pieces)


def passed_along(block, distance):
    count = lax.axis_size("pipe")
    route = [(i, i + distance) for i in range(count) if 0 <= i + distance < count]
    return lax.ppermute(block, "pipe", route)


def to_mirror(block, far):
    sections, size = lax.axis_size("pipe"), lax.axis_size("tensor")
    route = [
        (p * size + t, (sections - 2 - p) * size + (t + far * LANES) % size)
        for p in range(sections - 1)
        for t in range(size)
    ]
    return lax.ppermute(block, ("pipe", "tensor"), route)


def across_lanes(blocks):
    size = lax.axis_size("tensor")
    rows = [list(range(low, low + LANES)) for low in range(0, size, LANES)]
    return lax.all_to_all(
        blocks, "tensor", split_axis=1, concat_axis=1, axis_index_groups=rows, tiled=True
    )


def local(fwd_qkv, held_stash, d_out, positions, plan):
    me = lax.axis_index("tensor")
    group = me // LANES
    rows, heads, width = held_stash.shape[1:]
    mine = heads // (GROUPS * LANES)
    count = d_out.shape[1]

    def for_group(far):
        low = (group + far) % GROUPS * (LANES * mine)
        piece = lax.dynamic_slice_in_dim(held_stash[0], low, LANES * mine, 1)
        return piece.reshape(rows * LANES * mine, width)

    def by_lane(pieces):
        split = pieces.reshape(-1, rows, LANES, mine, width).transpose(0, 2, 3, 1, 4)
        return split

    def after(value, other):
        return lax.optimization_barrier((value, other))[0]

    first = stacked([to_mirror(for_group(far), far) for far in FIRST])
    crossed = across_lanes(by_lane(jnp.stack([for_group(far) for far in LATE])))
    late = stacked([to_mirror(crossed[n], far) for n, far in enumerate(LATE)])
    early = across_lanes(by_lane(first))
    packed = fwd_qkv[0].transpose(1, 0, 2)
    attn_out = jnp.stack([forward_of(head, plan, positions, packed) for head in range(mine)])
    which = jnp.broadcast_to(plan[0, 1].astype(jnp.bfloat16), (mine, 16, d_out.shape[3]))
    grad_out = passed_along(jnp.concatenate([after(d_out, attn_out)[0].transpose(1, 0, 2), which], axis=1), -1)
    to_next = passed_along(after(attn_out, grad_out), 1).transpose(1, 0, 2)
    place = group.astype(jnp.int32)[None]
    grads = backward_of(place, positions, grad_out, early, late)
    return to_next[None], grads.transpose(1, 0, 2)[None]


def solution(mesh):
    placed = (
        P("pipe", None, "tensor", None),
        P("pipe", "tensor", None, None),
        P("pipe", None, "tensor", None),
        P(),
        P("pipe", None),
    )
    return jax.shard_map(
        local,
        mesh=mesh,
        in_specs=placed,
        out_specs=(P("pipe", None, "tensor", None), P("pipe", None, "tensor", None)),
        check_vma=False,
    )
```
